32 devices in a mesh: pipe: 4 (over y, x), dp: 8 (over z, core).
Axes of the slice: x: 2, y: 2, z: 4, core: 2. Of those that a mesh axis runs over, the one named last changes fastest.
Arguments:
- hidden: float32 [64, 2048], P('dp', 'pipe'), may hold values from -6 to 6
- weight: float32 [8192, 2048], P(('pipe', 'dp')), may hold values from -0.375 to 0.375
- log_norm: float32 [64], replicated, may hold values from 14 to 17
- targets: int32 [64], replicated, may hold values from 0 to 8191
- loss_grad: float32 [64], replicated, may hold values from 0.5 to 2
Outputs:
- grad_hidden: float32 [64, 2048], P('dp', 'pipe')
- grad_weight: float32 [8192, 2048], P(('pipe', 'dp'))
The draws below stay inside these ranges and needn't reach their ends.
All inputs are finite; a program needn't handle non-finite values.
Results may differ from the reference program's by a relative error of at most 0.0003.
Values sent between devices are 32-bit elements; how exact they have to be, the bound alone decides.
A program may use at most 64 MiB of HBM per device.

```python
import jax
import jax.numpy as jnp
from jax import lax

D = 2048
TOKENS = 64
VOCAB = 8192
N_PIPE = 4


def set_ends(drawn, rng, least, largest):
    dims = drawn.shape
    index_at = [jax.random.randint(jax.random.fold_in(rng, axis), (), 0, dims[axis]) for axis in range(len(dims))]
    drawn = drawn.at[tuple(index_at)].set(least)
    longest = dims.index(max(dims))
    index_at[longest] = (index_at[longest] + 1) % dims[longest]
    return drawn.at[tuple(index_at)].set(largest)


def levels(key, dims, shards, smallest, high):
    loudness, own = 1.0, jax.random.fold_in(key, 6)
    for position, parts in shards:
        draws = jnp.exp(jax.random.uniform(jax.random.fold_in(own, position), (parts,), jnp.float32, smallest / len(shards), high / len(shards)))
        loudness = loudness * jnp.repeat(draws, dims[position] // parts).reshape([-1 if axis == position else 1 for axis in range(len(dims))])
    return loudness


def centred(stream_key, extent, scale, limit, pieces=(), kind=jnp.bfloat16):
    entries = scale * jax.random.normal(stream_key, extent, jnp.float32)
    if pieces:
        entries = entries * levels(stream_key, extent, pieces, -0.22, 0.18)
    return jnp.clip(entries, -limit, limit).astype(kind)


def setup_inputs(seed: int = 0) -> dict:
    key_list = jax.random.split(jax.random.key(seed), 6)
    hidden = centred(key_list[0], (TOKENS, D), 1.0, 6.0, ((0, 8), (1, 4)), jnp.float32)
    weight = centred(key_list[1], (VOCAB, D), (D // 9) ** -0.5, 0.375, ((0, 32),), jnp.float32)
    log_norm = jnp.clip(jax.random.uniform(key_list[2], (TOKENS,), jnp.float32, 14.0, 17.0), 14.0, 17.0)
    targets = set_ends(jax.random.randint(key_list[3], (TOKENS,), 0, VOCAB), jax.random.fold_in(key_list[3], 1), 0, VOCAB - 1).astype(jnp.int32)
    loss_grad = jnp.clip(jax.random.uniform(key_list[4], (TOKENS,), jnp.float32, 0.5, 2.0), 0.5, 2.0)
    return {"hidden": hidden, "weight": weight, "log_norm": log_norm, "targets": targets, "loss_grad": loss_grad}


def reference(hidden, weight, log_norm, targets, loss_grad):
    shard_rows = VOCAB // N_PIPE
    tiles = weight.reshape(N_PIPE, shard_rows, D)

    def advance(total, item):
        tile, which = item
        logits = jnp.dot(hidden, tile.T, precision=lax.Precision.HIGHEST, preferred_element_type=jnp.float32)
        prob = jnp.exp(logits - log_norm[:, None])
        columns = which * shard_rows + jnp.arange(shard_rows, dtype=jnp.int32)
        onehot = (targets[:, None] == columns[None, :]).astype(jnp.float32)
        dlogits = loss_grad[:, None] * (prob - onehot)
        total = total + jnp.dot(dlogits, tile, precision=lax.Precision.HIGHEST, preferred_element_type=jnp.float32)
        tile_grad = jnp.dot(dlogits.T, hidden, precision=lax.Precision.HIGHEST, preferred_element_type=jnp.float32)
        return total, tile_grad

    start_total = jnp.zeros((TOKENS, D), jnp.float32)
    grad_hidden, tile_grads = lax.scan(advance, start_total, (tiles, jnp.arange(N_PIPE, dtype=jnp.int32)))
    return grad_hidden, tile_grads.reshape(VOCAB, D)
```

```python
import functools

import jax
import jax.numpy as jnp
from jax import lax
from jax.experimental import pallas as pl
from jax.experimental.pallas import tpu as pltpu
from jax.sharding import PartitionSpec as P

F32, BF16 = jnp.float32, jnp.bfloat16
NT = (((1,), (1,)), ((), ()))


def partner(index, k, n):
    if n & (n - 1):
        return lax.rem(index + k, n)
    bit, out = 1, index
    while bit < n:
        if k & bit:
            out = out + bit - 2 * bit * lax.rem(index // bit, 2)
        bit *= 2
    return out


def source(index, k, n):
    if n & (n - 1):
        return lax.rem(index + n - k, n)
    return partner(index, k, n)


def split(x):
    high = x.astype(BF16)
    return high, (x - high.astype(F32)).astype(BF16)


def kernel(
    n_pipe, n_z, h_ref, w_hbm, ln_ref, tg_ref, lg_ref, gh_ref, gw_hbm,
    w_f32, w_hi, w_lo, hid, part, from_core, to_pipe, from_pipe, to_z, from_z, gw,
    w_sem, z_send, z_recv, p_send, p_recv, c_send, c_recv,
    rc_send, rc_recv, rp_send, rp_recv, rz_send, rz_recv, gw_sem,
):
    rows, feat = h_ref.shape
    vocab = w_hbm.shape[0]
    tokens = n_z * 2 * rows
    per_z = (n_pipe - 1) * n_z <= 64
    pipe, dp = lax.axis_index("pipe"), lax.axis_index("dp")
    z, core = dp // 2, lax.rem(dp, 2)
    other = 1 - core

    def at_z(k):
        return {"dp": partner(z, k, n_z) * 2 + core}

    def at_pipe(k):
        return {"pipe": partner(pipe, k, n_pipe)}

    sibling = {"dp": z * 2 + other}

    def remote(src, dst, send, recv, where):
        return pltpu.make_async_remote_copy(
            src_ref=src, dst_ref=dst, send_sem=send, recv_sem=recv, device_id=where,
            device_id_type=pl.DeviceIdType.MESH,
        )

    barrier = pltpu.get_barrier_semaphore()
    peers = [at_z(k) for k in range(1, n_z)] + [at_pipe(k) for k in range(1, n_pipe)] + [sibling]
    for peer in peers:
        pl.semaphore_signal(barrier, inc=1, device_id=peer, device_id_type=pl.DeviceIdType.MESH)
    w_copies = []
    for q in range(n_pipe):
        copy = pltpu.make_async_copy(w_hbm.at[:, pl.ds(q * feat, feat)], w_f32.at[q], w_sem.at[q])
        copy.start()
        w_copies.append(copy)
    hid[pipe, z, core] = h_ref[...]
    pl.semaphore_wait(barrier, len(peers))

    sends = []
    for k in range(1, n_z):
        block = hid.at[pipe, z, core]
        copy = remote(block, block, z_send.at[k], z_recv.at[k], at_z(k))
        copy.start()
        sends.append(copy)

    def over_pipe(j):
        for k in range(1, n_pipe):
            block = hid.at[pipe, source(z, j, n_z), core] if per_z else hid.at[pipe, :, core]
            copy = remote(block, block, p_send.at[k, j], p_recv.at[k, j], at_pipe(k))
            copy.start()
            sends.append(copy)

    def got_z(k):
        block = hid.at[pipe, source(z, k, n_z), core]
        remote(block, block, z_send.at[k], z_recv.at[k], at_z(k)).wait_recv()

    if per_z:
        over_pipe(0)
    for k in range(1, n_z):
        got_z(k)
        if per_z:
            over_pipe(k)
    if not per_z:
        over_pipe(0)

    def to_sibling(k):
        block = hid.at[source(pipe, k, n_pipe), :, core]
        copy = remote(block, block, c_send.at[k], c_recv.at[k], sibling)
        copy.start()
        sends.append(copy)

    to_sibling(0)
    for q in range(n_pipe):
        w_copies[q].wait()
        high, low = split(w_f32[q])
        w_hi[q] = high
        w_lo[q] = low
    for k in range(1, n_pipe):
        q = source(pipe, k, n_pipe)
        for j in range(n_z if per_z else 1):
            block = hid.at[q, source(z, j, n_z), core] if per_z else hid.at[q, :, core]
            remote(block, block, p_send.at[k, j], p_recv.at[k, j], at_pipe(k)).wait_recv()
        to_sibling(k)

    both = jnp.zeros((vocab, 2 * tokens), F32)
    low_part = jnp.zeros((vocab, tokens), F32)
    for k in range(n_pipe):
        q = source(pipe, k, n_pipe)
        block = hid.at[q, :, other]
        remote(block, block, c_send.at[k], c_recv.at[k], sibling).wait_recv()
        high, low = split(hid[q].reshape(tokens, feat))
        both += lax.dot_general(w_hi[q], jnp.concatenate([high, low], 0), NT, preferred_element_type=F32)
        low_part += lax.dot_general(w_lo[q], high, NT, preferred_element_type=F32)
    logits = both[:, :tokens] + both[:, tokens:] + low_part

    first = (pipe * n_z * 2 + dp) * vocab
    column = first + lax.broadcasted_iota(jnp.int32, (vocab, tokens), 0)
    onehot = (column == tg_ref[...]).astype(F32)
    dlogits = lg_ref[...] * (jnp.exp(logits - ln_ref[...]) - onehot)

    d_hi, d_lo = split(dlogits.T)
    d_both = jnp.concatenate([d_hi, d_lo], 0)
    order = list(range(n_pipe - 1, -1, -1))
    core_copies = {}
    for k in order:
        q = partner(pipe, k, n_pipe)
        whole = jnp.dot(d_both, w_hi[q], preferred_element_type=F32)
        total = whole[:tokens] + whole[tokens:] + jnp.dot(d_hi, w_lo[q], preferred_element_type=F32)
        part[k] = total.reshape(n_z, 2, rows, feat)
        copy = remote(part.at[k, :, other], from_core.at[k], rc_send.at[k], rc_recv.at[k], sibling)
        copy.start()
        core_copies[k] = copy
        sends.append(copy)
    pipe_copies = {}
    for k in order:
        core_copies[k].wait_recv()
        to_pipe[k] = part[k, :, core] + from_core[k]
        if k:
            copy = remote(to_pipe.at[k], from_pipe.at[k], rp_send.at[k], rp_recv.at[k], at_pipe(k))
            copy.start()
            pipe_copies[k] = copy
            sends.append(copy)

    t_hi, t_lo = split(dlogits)
    gw_copies = []

    def weight_grad(q):
        high, low = split(hid[q].reshape(tokens, feat))
        gw[q] = (
            jnp.dot(t_hi, high, preferred_element_type=F32)
            + jnp.dot(t_hi, low, preferred_element_type=F32)
            + jnp.dot(t_lo, high, preferred_element_type=F32)
        )
        copy = pltpu.make_async_copy(gw.at[q], gw_hbm.at[:, pl.ds(q * feat, feat)], gw_sem.at[q])
        copy.start()
        gw_copies.append(copy)

    half = (n_pipe + 1) // 2
    for q in range(half):
        weight_grad(q)
    total = to_pipe[0]
    for k in order[:-1]:
        pipe_copies[k].wait_recv()
        total += from_pipe[k]
    to_z[...] = total
    z_copies = []
    for k in range(1, n_z):
        copy = remote(to_z.at[partner(z, k, n_z)], from_z.at[k], rz_send.at[k], rz_recv.at[k], at_z(k))
        copy.start()
        z_copies.append(copy)
        sends.append(copy)
    for q in range(half, n_pipe):
        weight_grad(q)
    mine = to_z[z]
    for k in range(1, n_z):
        z_copies[k - 1].wait_recv()
        mine += from_z[k]
    gh_ref[...] = mine
    for copy in sends:
        copy.wait_send()
    for copy in gw_copies:
        copy.wait()


def on_device(n_pipe, n_dp, hidden, weight, log_norm, targets, loss_grad):
    rows, feat = hidden.shape
    vocab, width = weight.shape
    n_z = n_dp // 2
    dma = pltpu.SemaphoreType.DMA
    n_j = n_z if (n_pipe - 1) * n_z <= 64 else 1
    vmem = pl.BlockSpec(memory_space=pltpu.VMEM)
    hbm = pl.BlockSpec(memory_space=pl.ANY)
    return pl.pallas_call(
        functools.partial(kernel, n_pipe, n_z),
        out_shape=(jax.ShapeDtypeStruct((rows, feat), F32), jax.ShapeDtypeStruct((vocab, width), F32)),
        in_specs=[vmem, hbm, vmem, vmem, vmem],
        out_specs=(vmem, hbm),
        scratch_shapes=[
            pltpu.VMEM((n_pipe, vocab, feat), F32),
            pltpu.VMEM((n_pipe, vocab, feat), BF16),
            pltpu.VMEM((n_pipe, vocab, feat), BF16),
            pltpu.VMEM((n_pipe, n_z, 2, rows, feat), F32),
            pltpu.VMEM((n_pipe, n_z, 2, rows, feat), F32),
            pltpu.VMEM((n_pipe, n_z, rows, feat), F32),
            pltpu.VMEM((n_pipe, n_z, rows, feat), F32),
            pltpu.VMEM((n_pipe, n_z, rows, feat), F32),
            pltpu.VMEM((n_z, rows, feat), F32),
            pltpu.VMEM((n_z, rows, feat), F32),
            pltpu.VMEM((n_pipe, vocab, feat), F32),
            dma((n_pipe,)),
            dma((n_z,)), dma((n_z,)),
            dma((n_pipe, n_j)), dma((n_pipe, n_j)),
            dma((n_pipe,)), dma((n_pipe,)),
            dma((n_pipe,)), dma((n_pipe,)),
            dma((n_pipe,)), dma((n_pipe,)),
            dma((n_z,)), dma((n_z,)),
            dma((n_pipe,)),
        ],
        compiler_params=pltpu.CompilerParams(
            collective_id=0, has_side_effects=True, vmem_limit_bytes=48 * 2**20
        ),
    )(hidden, weight, log_norm[None], targets[None], loss_grad[None])


def solution(mesh):
    in_specs = (P("dp", "pipe"), P(("pipe", "dp"), None), P(), P(), P())
    out_specs = (P("dp", "pipe"), P(("pipe", "dp"), None))
    return jax.shard_map(
        functools.partial(on_device, mesh.shape["pipe"], mesh.shape["dp"]),
        mesh=mesh, in_specs=in_specs, out_specs=out_specs, check_vma=False,
    )
```

```python
import functools

import jax
import jax.numpy as jnp
from jax import lax
from jax.experimental import pallas as pl
from jax.experimental.pallas import tpu as pltpu
from jax.sharding import PartitionSpec as P

F32, BF16 = jnp.float32, jnp.bfloat16
NT = (((1,), (1,)), ((), ()))


def partner(index, k, n):
    if n & (n - 1):
        return lax.rem(index + k, n)
    bit, out = 1, index
    while bit < n:
        if k & bit:
            out = out + bit - 2 * bit * lax.rem(index // bit, 2)
        bit *= 2
    return out


def source(index, k, n):
    if n & (n - 1):
        return lax.rem(index + n - k, n)
    return partner(index, k, n)


def split(x):
    high = x.astype(BF16)
    return high, (x - high.astype(F32)).astype(BF16)


def kernel(
    n_pipe, n_z, h_hbm, w_hbm, ln_hbm, tg_hbm, lg_hbm, gh_ref, gw,
    w_f32, w_hi, w_lo, hid, ln_ref, tg_ref, lg_ref, part, from_core, to_pipe, from_pipe, to_z, from_z,
    w_sem, in_sem, z_send, z_recv, p_send, p_recv, c_send, c_recv,
    rc_send, rc_recv, rp_send, rp_recv, rz_send, rz_recv,
):
    rows, feat = h_hbm.shape
    vocab = w_hbm.shape[0]
    tokens = n_z * 2 * rows
    per_z = (n_pipe - 1) * n_z <= 64
    pipe, dp = lax.axis_index("pipe"), lax.axis_index("dp")
    z, core = dp // 2, lax.rem(dp, 2)
    other = 1 - core
    half = (n_pipe + 1) // 2

    def at_z(k):
        return {"dp": partner(z, k, n_z) * 2 + core}

    def at_pipe(k):
        return {"pipe": partner(pipe, k, n_pipe)}

    sibling = {"dp": z * 2 + other}

    def remote(src, dst, send, recv, where):
        return pltpu.make_async_remote_copy(
            src_ref=src, dst_ref=dst, send_sem=send, recv_sem=recv, device_id=where,
            device_id_type=pl.DeviceIdType.MESH,
        )

    barrier = pltpu.get_barrier_semaphore()
    peers = [at_z(k) for k in range(1, n_z)] + [at_pipe(k) for k in range(1, n_pipe)] + [sibling]
    for peer in peers:
        pl.semaphore_signal(barrier, inc=1, device_id=peer, device_id_type=pl.DeviceIdType.MESH)
    h_copy = pltpu.make_async_copy(h_hbm, hid.at[pipe, z, core], in_sem.at[0])
    h_copy.start()
    w_copies = []
    for q in range(n_pipe):
        copy = pltpu.make_async_copy(w_hbm.at[:, pl.ds(q * feat, feat)], w_f32.at[q], w_sem.at[q])
        copy.start()
        w_copies.append(copy)
    small_copies = []
    for i, (src, dst) in enumerate(((ln_hbm, ln_ref), (tg_hbm, tg_ref), (lg_hbm, lg_ref))):
        copy = pltpu.make_async_copy(src, dst, in_sem.at[i + 1])
        copy.start()
        small_copies.append(copy)
    h_copy.wait()
    pl.semaphore_wait(barrier, len(peers))

    sends = []
    for k in range(1, n_z):
        block = hid.at[pipe, z, core]
        copy = remote(block, block, z_send.at[k], z_recv.at[k], at_z(k))
        copy.start()
        sends.append(copy)

    def over_pipe(j):
        for k in range(1, n_pipe):
            block = hid.at[pipe, source(z, j, n_z), core] if per_z else hid.at[pipe, :, core]
            copy = remote(block, block, p_send.at[k, j], p_recv.at[k, j], at_pipe(k))
            copy.start()
            sends.append(copy)

    def got_z(k):
        block = hid.at[pipe, source(z, k, n_z), core]
        remote(block, block, z_send.at[k], z_recv.at[k], at_z(k)).wait_recv()

    def split_weight(q):
        w_copies[q].wait()
        high, low = split(w_f32[q])
        w_hi[q] = high
        w_lo[q] = low

    if per_z:
        over_pipe(0)
    for q in range(half):
        split_weight(q)
    for k in range(1, n_z):
        got_z(k)
        if per_z:
            over_pipe(k)
    if not per_z:
        over_pipe(0)

    def to_sibling(k):
        block = hid.at[source(pipe, k, n_pipe), :, core]
        copy = remote(block, block, c_send.at[k], c_recv.at[k], sibling)
        copy.start()
        sends.append(copy)

    to_sibling(0)
    for q in range(half, n_pipe):
        split_weight(q)
    for copy in small_copies:
        copy.wait()
    for k in range(1, n_pipe):
        q = source(pipe, k, n_pipe)
        for j in range(n_z if per_z else 1):
            block = hid.at[q, source(z, j, n_z), core] if per_z else hid.at[q, :, core]
            remote(block, block, p_send.at[k, j], p_recv.at[k, j], at_pipe(k)).wait_recv()
        to_sibling(k)

    both = jnp.zeros((vocab, 2 * tokens), F32)
    low_part = jnp.zeros((vocab, tokens), F32)
    for k in range(n_pipe):
        q = source(pipe, k, n_pipe)
        block = hid.at[q, :, other]
        remote(block, block, c_send.at[k], c_recv.at[k], sibling).wait_recv()
        high, low = split(hid[q].reshape(tokens, feat))
        both += lax.dot_general(w_hi[q], jnp.concatenate([high, low], 0), NT, preferred_element_type=F32)
        low_part += lax.dot_general(w_lo[q], high, NT, preferred_element_type=F32)
    logits = both[:, :tokens] + both[:, tokens:] + low_part

    first = (pipe * n_z * 2 + dp) * vocab
    column = first + lax.broadcasted_iota(jnp.int32, (vocab, tokens), 0)
    onehot = (column == tg_ref[...]).astype(F32)
    dlogits = lg_ref[...] * (jnp.exp(logits - ln_ref[...]) - onehot)

    d_hi, d_lo = split(dlogits.T)
    d_both = jnp.concatenate([d_hi, d_lo], 0)
    order = list(range(n_pipe - 1, -1, -1))
    core_copies = {}
    for k in order:
        q = partner(pipe, k, n_pipe)
        whole = jnp.dot(d_both, w_hi[q], preferred_element_type=F32)
        total = whole[:tokens] + whole[tokens:] + jnp.dot(d_hi, w_lo[q], preferred_element_type=F32)
        part[k] = total.reshape(n_z, 2, rows, feat)
        copy = remote(part.at[k, :, other], from_core.at[k], rc_send.at[k], rc_recv.at[k], sibling)
        copy.start()
        core_copies[k] = copy
        sends.append(copy)
    pipe_copies = {}
    for k in order:
        core_copies[k].wait_recv()
        to_pipe[k] = part[k, :, core] + from_core[k]
        if k:
            copy = remote(to_pipe.at[k], from_pipe.at[k], rp_send.at[k], rp_recv.at[k], at_pipe(k))
            copy.start()
            pipe_copies[k] = copy
            sends.append(copy)

    t_hi, t_lo = split(dlogits)

    def weight_grad(q):
        high, low = split(hid[q].reshape(tokens, feat))
        gw[q] = (
            jnp.dot(t_hi, high, preferred_element_type=F32)
            + jnp.dot(t_hi, low, preferred_element_type=F32)
            + jnp.dot(t_lo, high, preferred_element_type=F32)
        )

    for q in range(half):
        weight_grad(q)
    total = to_pipe[0]
    for k in order[:-1]:
        pipe_copies[k].wait_recv()
        total += from_pipe[k]
    to_z[...] = total
    z_copies = []
    for k in range(1, n_z):
        copy = remote(to_z.at[partner(z, k, n_z)], from_z.at[k], rz_send.at[k], rz_recv.at[k], at_z(k))
        copy.start()
        z_copies.append(copy)
        sends.append(copy)
    for q in range(half, n_pipe):
        weight_grad(q)
    mine = to_z[z]
    for k in range(1, n_z):
        z_copies[k - 1].wait_recv()
        mine += from_z[k]
    gh_ref[...] = mine
    for copy in sends:
        copy.wait_send()


def store_kernel(n_pipe, gh_ref, gw_ref, gh_hbm, gw_hbm, sem):
    feat = gw_ref.shape[2]
    copies = [
        pltpu.make_async_copy(gw_ref.at[q], gw_hbm.at[:, pl.ds(q * feat, feat)], sem.at[q]) for q in range(n_pipe)
    ]
    copies.append(pltpu.make_async_copy(gh_ref, gh_hbm, sem.at[n_pipe]))
    for copy in copies:
        copy.start()
    for copy in copies:
        copy.wait()


def in_hbm(x):
    return pltpu.with_memory_space_constraint(x, pltpu.HBM)


def in_vmem(x):
    return pltpu.with_memory_space_constraint(x, pltpu.VMEM)


def on_device(n_pipe, n_dp, hidden, weight, log_norm, targets, loss_grad):
    rows, feat = hidden.shape
    vocab, width = weight.shape
    n_z = n_dp // 2
    tokens = n_dp * rows
    dma = pltpu.SemaphoreType.DMA
    n_j = n_z if (n_pipe - 1) * n_z <= 64 else 1
    vmem = pl.BlockSpec(memory_space=pltpu.VMEM)
    hbm = pl.BlockSpec(memory_space=pltpu.HBM)
    hidden_grad, weight_grad = pl.pallas_call(
        functools.partial(kernel, n_pipe, n_z),
        out_shape=(pltpu.VMEM((rows, feat), F32), pltpu.VMEM((n_pipe, vocab, feat), F32)),
        in_specs=[hbm] * 5,
        out_specs=(vmem, vmem),
        scratch_shapes=[
            pltpu.VMEM((n_pipe, vocab, feat), F32),
            pltpu.VMEM((n_pipe, vocab, feat), BF16),
            pltpu.VMEM((n_pipe, vocab, feat), BF16),
            pltpu.VMEM((n_pipe, n_z, 2, rows, feat), F32),
            pltpu.VMEM((1, tokens), F32),
            pltpu.VMEM((1, tokens), jnp.int32),
            pltpu.VMEM((1, tokens), F32),
            pltpu.VMEM((n_pipe, n_z, 2, rows, feat), F32),
            pltpu.VMEM((n_pipe, n_z, rows, feat), F32),
            pltpu.VMEM((n_pipe, n_z, rows, feat), F32),
            pltpu.VMEM((n_pipe, n_z, rows, feat), F32),
            pltpu.VMEM((n_z, rows, feat), F32),
            pltpu.VMEM((n_z, rows, feat), F32),
            dma((n_pipe,)), dma((4,)),
            dma((n_z,)), dma((n_z,)),
            dma((n_pipe, n_j)), dma((n_pipe, n_j)),
            dma((n_pipe,)), dma((n_pipe,)),
            dma((n_pipe,)), dma((n_pipe,)),
            dma((n_pipe,)), dma((n_pipe,)),
            dma((n_z,)), dma((n_z,)),
        ],
        compiler_params=pltpu.CompilerParams(
            collective_id=0, has_side_effects=True, vmem_limit_bytes=32 * 2**20
        ),
    )(*(in_hbm(x) for x in (hidden, weight, log_norm[None], targets[None], loss_grad[None])))
    return pl.pallas_call(
        functools.partial(store_kernel, n_pipe),
        out_shape=(jax.ShapeDtypeStruct((rows, feat), F32), jax.ShapeDtypeStruct((vocab, width), F32)),
        in_specs=[vmem, vmem],
        out_specs=(hbm, hbm),
        scratch_shapes=[dma((n_pipe + 1,))],
    )(in_vmem(hidden_grad), in_vmem(weight_grad))


def solution(mesh):
    in_specs = (P("dp", "pipe"), P(("pipe", "dp"), None), P(), P(), P())
    out_specs = (P("dp", "pipe"), P(("pipe", "dp"), None))
    return jax.shard_map(
        functools.partial(on_device, mesh.shape["pipe"], mesh.shape["dp"]),
        mesh=mesh, in_specs=in_specs, out_specs=out_specs, check_vma=False,
    )
```

```python
import functools

import jax
import jax.numpy as jnp
from jax import lax
from jax.experimental import pallas as pl
from jax.experimental.pallas import tpu as pltpu
from jax.sharding import PartitionSpec as P

F32, BF16 = jnp.float32, jnp.bfloat16
NT = (((1,), (1,)), ((), ()))


def partner(index, k, n):
    if n & (n - 1):
        return lax.rem(index + k, n)
    bit, out = 1, index
    while bit < n:
        if k & bit:
            out = out + bit - 2 * bit * lax.rem(index // bit, 2)
        bit *= 2
    return out


def source(index, k, n):
    if n & (n - 1):
        return lax.rem(index + n - k, n)
    return partner(index, k, n)


def split(x):
    high = x.astype(BF16)
    return high, (x - high.astype(F32)).astype(BF16)


def kernel(
    n_pipe, n_z, h_hbm, w_hbm, ln_hbm, tg_hbm, lg_hbm, gh_ref, gw,
    w_f32, w_hi, w_lo, hid, ln_ref, tg_ref, lg_ref, part, from_core, to_pipe, from_pipe, to_z, from_z,
    w_sem, in_sem, z_send, z_recv, p_send, p_recv, c_send, c_recv,
    rc_send, rc_recv, rp_send, rp_recv, rz_send, rz_recv,
):
    rows, feat = h_hbm.shape
    vocab = w_hbm.shape[0]
    tokens = n_z * 2 * rows
    per_z = (n_pipe - 1) * n_z <= 64
    pipe, dp = lax.axis_index("pipe"), lax.axis_index("dp")
    z, core = dp // 2, lax.rem(dp, 2)
    other = 1 - core
    half = (n_pipe + 1) // 2

    def at_z(k):
        return {"dp": partner(z, k, n_z) * 2 + core}

    def at_pipe(k):
        return {"pipe": partner(pipe, k, n_pipe)}

    sibling = {"dp": z * 2 + other}

    def remote(src, dst, send, recv, where):
        return pltpu.make_async_remote_copy(
            src_ref=src, dst_ref=dst, send_sem=send, recv_sem=recv, device_id=where,
            device_id_type=pl.DeviceIdType.MESH,
        )

    barrier = pltpu.get_barrier_semaphore()
    peers = [at_z(k) for k in range(1, n_z)] + [at_pipe(k) for k in range(1, n_pipe)] + [sibling]
    for peer in peers:
        pl.semaphore_signal(barrier, inc=1, device_id=peer, device_id_type=pl.DeviceIdType.MESH)
    h_copy = pltpu.make_async_copy(h_hbm, hid.at[pipe, z, core], in_sem.at[0])
    h_copy.start()
    w_copies = []
    for q in range(n_pipe):
        copy = pltpu.make_async_copy(w_hbm.at[:, pl.ds(q * feat, feat)], w_f32.at[q], w_sem.at[q])
        copy.start()
        w_copies.append(copy)
    small_copies = []
    for i, (src, dst) in enumerate(((ln_hbm, ln_ref), (tg_hbm, tg_ref), (lg_hbm, lg_ref))):
        copy = pltpu.make_async_copy(src, dst, in_sem.at[i + 1])
        copy.start()
        small_copies.append(copy)
    h_copy.wait()
    pl.semaphore_wait(barrier, len(peers))

    sends = []
    for k in range(n_z - 1, 0, -1):
        block = hid.at[pipe, z, core]
        copy = remote(block, block, z_send.at[k], z_recv.at[k], at_z(k))
        copy.start()
        sends.append(copy)

    def over_pipe(j):
        for k in range(1, n_pipe):
            block = hid.at[pipe, source(z, j, n_z), core] if per_z else hid.at[pipe, :, core]
            copy = remote(block, block, p_send.at[k, j], p_recv.at[k, j], at_pipe(k))
            copy.start()
            sends.append(copy)

    def got_z(k):
        block = hid.at[pipe, source(z, k, n_z), core]
        remote(block, block, z_send.at[k], z_recv.at[k], at_z(k)).wait_recv()

    def split_weight(q):
        w_copies[q].wait()
        high, low = split(w_f32[q])
        w_hi[q] = high
        w_lo[q] = low

    if per_z:
        over_pipe(0)
    for q in range(half):
        split_weight(q)
    for k in range(1, n_z):
        got_z(k)
        if per_z:
            over_pipe(k)
    if not per_z:
        over_pipe(0)

    def to_sibling(k):
        block = hid.at[source(pipe, k, n_pipe), :, core]
        copy = remote(block, block, c_send.at[k], c_recv.at[k], sibling)
        copy.start()
        sends.append(copy)

    to_sibling(0)
    for q in range(half, n_pipe):
        split_weight(q)
    for copy in small_copies:
        copy.wait()
    both = jnp.zeros((vocab, 2 * tokens), F32)
    low_part = jnp.zeros((vocab, tokens), F32)
    for k in range(1, n_pipe + 1):
        if k < n_pipe:
            q = source(pipe, k, n_pipe)
            for j in range(n_z if per_z else 1):
                block = hid.at[q, source(z, j, n_z), core] if per_z else hid.at[q, :, core]
                remote(block, block, p_send.at[k, j], p_recv.at[k, j], at_pipe(k)).wait_recv()
            to_sibling(k)
    for k in range(1, n_pipe + 1):
        q = source(pipe, k - 1, n_pipe)
        block = hid.at[q, :, other]
        remote(block, block, c_send.at[k - 1], c_recv.at[k - 1], sibling).wait_recv()
        high, low = split(hid[q].reshape(tokens, feat))
        both += lax.dot_general(w_hi[q], jnp.concatenate([high, low], 0), NT, preferred_element_type=F32)
        low_part += lax.dot_general(w_lo[q], high, NT, preferred_element_type=F32)
    logits = both[:, :tokens] + both[:, tokens:] + low_part

    first = (pipe * n_z * 2 + dp) * vocab
    column = first + lax.broadcasted_iota(jnp.int32, (vocab, tokens), 0)
    onehot = (column == tg_ref[...]).astype(F32)
    dlogits = lg_ref[...] * (jnp.exp(logits - ln_ref[...]) - onehot)

    d_hi, d_lo = split(dlogits.T)
    d_both = jnp.concatenate([d_hi, d_lo], 0)
    order = list(range(n_pipe - 1, -1, -1))
    z_order = list(range(n_z - 1, -1, -1)) if per_z else [0]
    core_copies, pipe_copies = {}, {}

    def on_to_pipe(k):
        core_copies[k].wait_recv()
        to_pipe[k] = part[k, :, core] + from_core[k]
        if k:
            for j in z_order:
                piece = (k, partner(z, j, n_z)) if per_z else (k,)
                copy = remote(to_pipe.at[piece], from_pipe.at[piece], rp_send.at[k, j], rp_recv.at[k, j], at_pipe(k))
                copy.start()
                pipe_copies[k, j] = copy
                sends.append(copy)

    for n, k in enumerate(order):
        q = partner(pipe, k, n_pipe)
        whole = jnp.dot(d_both, w_hi[q], preferred_element_type=F32)
        total = whole[:tokens] + whole[tokens:] + jnp.dot(d_hi, w_lo[q], preferred_element_type=F32)
        part[k] = total.reshape(n_z, 2, rows, feat)
        copy = remote(part.at[k, :, other], from_core.at[k], rc_send.at[k], rc_recv.at[k], sibling)
        copy.start()
        core_copies[k] = copy
        sends.append(copy)
        if n >= 2:
            on_to_pipe(order[n - 2])
    for k in order[-2:]:
        on_to_pipe(k)

    t_hi, t_lo = split(dlogits)

    def weight_grad(q):
        high, low = split(hid[q].reshape(tokens, feat))
        gw[:, q * feat : (q + 1) * feat] = (
            jnp.dot(t_hi, high, preferred_element_type=F32)
            + jnp.dot(t_hi, low, preferred_element_type=F32)
            + jnp.dot(t_lo, high, preferred_element_type=F32)
        )

    for q in range(half):
        weight_grad(q)
    z_copies = {}
    for j in range(n_z - 1, -1, -1):
        at = partner(z, j, n_z)
        total = to_pipe[0, at]
        for k in order[:-1]:
            if per_z or j == n_z - 1:
                pipe_copies[k, j if per_z else 0].wait_recv()
            total += from_pipe[k, at]
        to_z[at] = total
        if j:
            copy = remote(to_z.at[at], from_z.at[j], rz_send.at[j], rz_recv.at[j], at_z(j))
            copy.start()
            z_copies[j] = copy
            sends.append(copy)
    for q in range(half, n_pipe):
        weight_grad(q)
    mine = to_z[z]
    for k in range(1, n_z):
        z_copies[k].wait_recv()
        mine += from_z[k]
    gh_ref[...] = mine
    for copy in sends:
        copy.wait_send()


def store_kernel(pieces, gh_ref, gw_ref, gh_hbm, gw_hbm, sem):
    rows = gw_ref.shape[0] // pieces
    copies = [pltpu.make_async_copy(gh_ref, gh_hbm, sem.at[pieces])]
    for i in range(pieces):
        block = pl.ds(i * rows, rows)
        copies.append(pltpu.make_async_copy(gw_ref.at[block], gw_hbm.at[block], sem.at[i]))
    for copy in copies:
        copy.start()
    for copy in copies:
        copy.wait()


def in_hbm(x):
    return pltpu.with_memory_space_constraint(x, pltpu.HBM)


def in_vmem(x):
    return pltpu.with_memory_space_constraint(x, pltpu.VMEM)


def on_device(n_pipe, n_dp, hidden, weight, log_norm, targets, loss_grad):
    rows, feat = hidden.shape
    vocab, width = weight.shape
    n_z = n_dp // 2
    tokens = n_dp * rows
    pieces = 8 if vocab % 64 == 0 else 1
    dma = pltpu.SemaphoreType.DMA
    n_j = n_z if (n_pipe - 1) * n_z <= 64 else 1
    vmem = pl.BlockSpec(memory_space=pltpu.VMEM)
    hbm = pl.BlockSpec(memory_space=pltpu.HBM)
    hidden_grad, weight_grad = pl.pallas_call(
        functools.partial(kernel, n_pipe, n_z),
        out_shape=(pltpu.VMEM((rows, feat), F32), pltpu.VMEM((vocab, width), F32)),
        in_specs=[hbm] * 5,
        out_specs=(vmem, vmem),
        scratch_shapes=[
            pltpu.VMEM((n_pipe, vocab, feat), F32),
            pltpu.VMEM((n_pipe, vocab, feat), BF16),
            pltpu.VMEM((n_pipe, vocab, feat), BF16),
            pltpu.VMEM((n_pipe, n_z, 2, rows, feat), F32),
            pltpu.VMEM((1, tokens), F32),
            pltpu.VMEM((1, tokens), jnp.int32),
            pltpu.VMEM((1, tokens), F32),
            pltpu.VMEM((n_pipe, n_z, 2, rows, feat), F32),
            pltpu.VMEM((n_pipe, n_z, rows, feat), F32),
            pltpu.VMEM((n_pipe, n_z, rows, feat), F32),
            pltpu.VMEM((n_pipe, n_z, rows, feat), F32),
            pltpu.VMEM((n_z, rows, feat), F32),
            pltpu.VMEM((n_z, rows, feat), F32),
            dma((n_pipe,)), dma((4,)),
            dma((n_z,)), dma((n_z,)),
            dma((n_pipe, n_j)), dma((n_pipe, n_j)),
            dma((n_pipe,)), dma((n_pipe,)),
            dma((n_pipe,)), dma((n_pipe,)),
            dma((n_pipe, n_j)), dma((n_pipe, n_j)),
            dma((n_z,)), dma((n_z,)),
        ],
        compiler_params=pltpu.CompilerParams(
            collective_id=0, has_side_effects=True, vmem_limit_bytes=32 * 2**20
        ),
    )(*(in_hbm(x) for x in (hidden, weight, log_norm[None], targets[None], loss_grad[None])))
    return pl.pallas_call(
        functools.partial(store_kernel, pieces),
        out_shape=(jax.ShapeDtypeStruct((rows, feat), F32), jax.ShapeDtypeStruct((vocab, width), F32)),
        in_specs=[vmem, vmem],
        out_specs=(hbm, hbm),
        scratch_shapes=[dma((pieces + 1,))],
    )(in_vmem(hidden_grad), in_vmem(weight_grad))


def solution(mesh):
    in_specs = (P("dp", "pipe"), P(("pipe", "dp"), None), P(), P(), P())
    out_specs = (P("dp", "pipe"), P(("pipe", "dp"), None))
    return jax.shard_map(
        functools.partial(on_device, mesh.shape["pipe"], mesh.shape["dp"]),
        mesh=mesh, in_specs=in_specs, out_specs=out_specs, check_vma=False,
    )
```

```python
import functools

import jax
import jax.numpy as jnp
from jax import lax
from jax.experimental import pallas as pl
from jax.experimental.pallas import tpu as pltpu
from jax.sharding import PartitionSpec as P

F32, BF16 = jnp.float32, jnp.bfloat16
NT = (((1,), (1,)), ((), ()))


def partner(index, k, n):
    if n & (n - 1):
        return lax.rem(index + k, n)
    bit, out = 1, index
    while bit < n:
        if k & bit:
            out = out + bit - 2 * bit * lax.rem(index // bit, 2)
        bit *= 2
    return out


def source(index, k, n):
    if n & (n - 1):
        return lax.rem(index + n - k, n)
    return partner(index, k, n)


def split(x):
    high = x.astype(BF16)
    return high, (x - high.astype(F32)).astype(BF16)


def kernel(
    n_pipe, n_z, h_hbm, w_hbm, ln_hbm, tg_hbm, lg_hbm, gh_ref, gw,
    w_f32, w_hi, w_lo, hid, ln_ref, tg_ref, lg_ref, part, from_core, to_pipe, from_pipe, to_z, from_z,
    w_sem, in_sem, z_send, z_recv, p_send, p_recv, c_send, c_recv,
    rc_send, rc_recv, rp_send, rp_recv, rz_send, rz_recv,
):
    rows, feat = h_hbm.shape
    vocab = w_hbm.shape[0]
    tokens = n_z * 2 * rows
    per_z = (n_pipe - 1) * n_z <= 64
    pipe, dp = lax.axis_index("pipe"), lax.axis_index("dp")
    z, core = dp // 2, lax.rem(dp, 2)
    other = 1 - core
    half = (n_pipe + 1) // 2

    def at_z(k):
        return {"dp": partner(z, k, n_z) * 2 + core}

    def at_pipe(k):
        return {"pipe": partner(pipe, k, n_pipe)}

    sibling = {"dp": z * 2 + other}

    def remote(src, dst, send, recv, where):
        return pltpu.make_async_remote_copy(
            src_ref=src, dst_ref=dst, send_sem=send, recv_sem=recv, device_id=where,
            device_id_type=pl.DeviceIdType.MESH,
        )

    barrier = pltpu.get_barrier_semaphore()
    peers = [at_z(k) for k in range(1, n_z)] + [at_pipe(k) for k in range(1, n_pipe)] + [sibling]
    for peer in peers:
        pl.semaphore_signal(barrier, inc=1, device_id=peer, device_id_type=pl.DeviceIdType.MESH)
    h_copy = pltpu.make_async_copy(h_hbm, hid.at[pipe, z, core], in_sem.at[0])
    h_copy.start()
    w_copies = []
    for q in range(n_pipe):
        copy = pltpu.make_async_copy(w_hbm.at[:, pl.ds(q * feat, feat)], w_f32.at[q], w_sem.at[q])
        copy.start()
        w_copies.append(copy)
    small_copies = []
    for i, (src, dst) in enumerate(((ln_hbm, ln_ref), (tg_hbm, tg_ref), (lg_hbm, lg_ref))):
        copy = pltpu.make_async_copy(src, dst, in_sem.at[i + 1])
        copy.start()
        small_copies.append(copy)
    h_copy.wait()
    pl.semaphore_wait(barrier, len(peers))

    sends = []
    for k in range(n_z - 1, 0, -1):
        block = hid.at[pipe, z, core]
        copy = remote(block, block, z_send.at[k], z_recv.at[k], at_z(k))
        copy.start()
        sends.append(copy)

    def over_pipe(j):
        for k in range(n_pipe - 1, 0, -1):
            block = hid.at[pipe, source(z, j, n_z), core] if per_z else hid.at[pipe, :, core]
            copy = remote(block, block, p_send.at[k, j], p_recv.at[k, j], at_pipe(k))
            copy.start()
            sends.append(copy)

    def got_z(k):
        block = hid.at[pipe, source(z, k, n_z), core]
        remote(block, block, z_send.at[k], z_recv.at[k], at_z(k)).wait_recv()

    def split_weight(q):
        w_copies[q].wait()
        high, low = split(w_f32[q])
        w_hi[q] = high
        w_lo[q] = low

    if per_z:
        over_pipe(0)
    for q in range(half):
        split_weight(q)
    for k in range(1, n_z):
        got_z(k)
        if per_z:
            over_pipe(k)
    if not per_z:
        over_pipe(0)

    def to_sibling(k):
        block = hid.at[source(pipe, k, n_pipe), :, core]
        copy = remote(block, block, c_send.at[k], c_recv.at[k], sibling)
        copy.start()
        sends.append(copy)

    to_sibling(0)
    for q in range(half, n_pipe):
        split_weight(q)
    for copy in small_copies:
        copy.wait()
    both = jnp.zeros((vocab, 2 * tokens), F32)
    low_part = jnp.zeros((vocab, tokens), F32)
    for k in range(1, n_pipe + 1):
        if k < n_pipe:
            q = source(pipe, k, n_pipe)
            for j in range(n_z if per_z else 1):
                block = hid.at[q, source(z, j, n_z), core] if per_z else hid.at[q, :, core]
                remote(block, block, p_send.at[k, j], p_recv.at[k, j], at_pipe(k)).wait_recv()
            to_sibling(k)
    for k in range(1, n_pipe + 1):
        q = source(pipe, k - 1, n_pipe)
        block = hid.at[q, :, other]
        remote(block, block, c_send.at[k - 1], c_recv.at[k - 1], sibling).wait_recv()
        high, low = split(hid[q].reshape(tokens, feat))
        both += lax.dot_general(w_hi[q], jnp.concatenate([high, low], 0), NT, preferred_element_type=F32)
        low_part += lax.dot_general(w_lo[q], high, NT, preferred_element_type=F32)
    logits = both[:, :tokens] + both[:, tokens:] + low_part

    first = (pipe * n_z * 2 + dp) * vocab
    column = first + lax.broadcasted_iota(jnp.int32, (vocab, tokens), 0)
    onehot = (column == tg_ref[...]).astype(F32)
    dlogits = lg_ref[...] * (jnp.exp(logits - ln_ref[...]) - onehot)

    d_hi, d_lo = split(dlogits.T)
    d_both = jnp.concatenate([d_hi, d_lo], 0)
    order = list(range(n_pipe - 1, -1, -1))
    z_order = list(range(n_z - 1, -1, -1)) if per_z else [0]
    core_copies, pipe_copies = {}, {}

    def on_to_pipe(k):
        core_copies[k].wait_recv()
        to_pipe[k] = part[k, :, core] + from_core[k]
        if k:
            for j in z_order:
                piece = (k, partner(z, j, n_z)) if per_z else (k,)
                copy = remote(to_pipe.at[piece], from_pipe.at[piece], rp_send.at[k, j], rp_recv.at[k, j], at_pipe(k))
                copy.start()
                pipe_copies[k, j] = copy
                sends.append(copy)

    for n, k in enumerate(order):
        q = partner(pipe, k, n_pipe)
        whole = jnp.dot(d_both, w_hi[q], preferred_element_type=F32)
        total = whole[:tokens] + whole[tokens:] + jnp.dot(d_hi, w_lo[q], preferred_element_type=F32)
        part[k] = total.reshape(n_z, 2, rows, feat)
        copy = remote(part.at[k, :, other], from_core.at[k], rc_send.at[k], rc_recv.at[k], sibling)
        copy.start()
        core_copies[k] = copy
        sends.append(copy)
        if n >= 2:
            on_to_pipe(order[n - 2])
    for k in order[-2:]:
        on_to_pipe(k)

    t_hi, t_lo = split(dlogits)

    def weight_grad(q):
        high, low = split(hid[q].reshape(tokens, feat))
        gw[:, q * feat : (q + 1) * feat] = (
            jnp.dot(t_hi, high, preferred_element_type=F32)
            + jnp.dot(t_hi, low, preferred_element_type=F32)
            + jnp.dot(t_lo, high, preferred_element_type=F32)
        )

    for q in range(half):
        weight_grad(q)
    z_copies = {}
    for j in range(n_z - 1, -1, -1):
        at = partner(z, j, n_z)
        total = to_pipe[0, at]
        for k in order[:-1]:
            if per_z or j == n_z - 1:
                pipe_copies[k, j if per_z else 0].wait_recv()
            total += from_pipe[k, at]
        to_z[at] = total
        if j:
            copy = remote(to_z.at[at], from_z.at[j], rz_send.at[j], rz_recv.at[j], at_z(j))
            copy.start()
            z_copies[j] = copy
            sends.append(copy)
    for q in range(half, n_pipe):
        weight_grad(q)
    mine = to_z[z]
    for k in range(1, n_z):
        z_copies[k].wait_recv()
        mine += from_z[k]
    gh_ref[...] = mine
    for copy in sends:
        copy.wait_send()


def store_kernel(pieces, gh_ref, gw_ref, gh_hbm, gw_hbm, sem):
    rows = gw_ref.shape[0] // pieces
    copies = [pltpu.make_async_copy(gh_ref, gh_hbm, sem.at[pieces])]
    for i in range(pieces):
        block = pl.ds(i * rows, rows)
        copies.append(pltpu.make_async_copy(gw_ref.at[block], gw_hbm.at[block], sem.at[i]))
    for copy in copies:
        copy.start()
    for copy in copies:
        copy.wait()


def in_hbm(x):
    return pltpu.with_memory_space_constraint(x, pltpu.HBM)


def in_vmem(x):
    return pltpu.with_memory_space_constraint(x, pltpu.VMEM)


def on_device(n_pipe, n_dp, hidden, weight, log_norm, targets, loss_grad):
    rows, feat = hidden.shape
    vocab, width = weight.shape
    n_z = n_dp // 2
    tokens = n_dp * rows
    pieces = 8 if vocab % 64 == 0 else 1
    dma = pltpu.SemaphoreType.DMA
    n_j = n_z if (n_pipe - 1) * n_z <= 64 else 1
    vmem = pl.BlockSpec(memory_space=pltpu.VMEM)
    hbm = pl.BlockSpec(memory_space=pltpu.HBM)
    hidden_grad, weight_grad = pl.pallas_call(
        functools.partial(kernel, n_pipe, n_z),
        out_shape=(pltpu.VMEM((rows, feat), F32), pltpu.VMEM((vocab, width), F32)),
        in_specs=[hbm] * 5,
        out_specs=(vmem, vmem),
        scratch_shapes=[
            pltpu.VMEM((n_pipe, vocab, feat), F32),
            pltpu.VMEM((n_pipe, vocab, feat), BF16),
            pltpu.VMEM((n_pipe, vocab, feat), BF16),
            pltpu.VMEM((n_pipe, n_z, 2, rows, feat), F32),
            pltpu.VMEM((1, tokens), F32),
            pltpu.VMEM((1, tokens), jnp.int32),
            pltpu.VMEM((1, tokens), F32),
            pltpu.VMEM((n_pipe, n_z, 2, rows, feat), F32),
            pltpu.VMEM((n_pipe, n_z, rows, feat), F32),
            pltpu.VMEM((n_pipe, n_z, rows, feat), F32),
            pltpu.VMEM((n_pipe, n_z, rows, feat), F32),
            pltpu.VMEM((n_z, rows, feat), F32),
            pltpu.VMEM((n_z, rows, feat), F32),
            dma((n_pipe,)), dma((4,)),
            dma((n_z,)), dma((n_z,)),
            dma((n_pipe, n_j)), dma((n_pipe, n_j)),
            dma((n_pipe,)), dma((n_pipe,)),
            dma((n_pipe,)), dma((n_pipe,)),
            dma((n_pipe, n_j)), dma((n_pipe, n_j)),
            dma((n_z,)), dma((n_z,)),
        ],
        compiler_params=pltpu.CompilerParams(
            collective_id=0, has_side_effects=True, vmem_limit_bytes=32 * 2**20
        ),
    )(*(in_hbm(x) for x in (hidden, weight, log_norm[None], targets[None], loss_grad[None])))
    return pl.pallas_call(
        functools.partial(store_kernel, pieces),
        out_shape=(jax.ShapeDtypeStruct((rows, feat), F32), jax.ShapeDtypeStruct((vocab, width), F32)),
        in_specs=[vmem, vmem],
        out_specs=(hbm, hbm),
        scratch_shapes=[dma((pieces + 1,))],
    )(in_vmem(hidden_grad), in_vmem(weight_grad))


def solution(mesh):
    in_specs = (P("dp", "pipe"), P(("pipe", "dp"), None), P(), P(), P())
    out_specs = (P("dp", "pipe"), P(("pipe", "dp"), None))
    return jax.shard_map(
        functools.partial(on_device, mesh.shape["pipe"], mesh.shape["dp"]),
        mesh=mesh, in_specs=in_specs, out_specs=out_specs, check_vma=False,
    )
```
